32 devices in a mesh: groups: 2 (over y), wide: 4 (over z), dp: 2 (over x), expert: 2 (over core).
Axes of the slice: x: 2, y: 2, z: 4, core: 2. Of those that a mesh axis runs over, the one named last changes fastest.
Arguments:
- tokens: bfloat16 [2, 2048, 4096], P('expert', ('groups', 'wide', 'dp')), parts along dimension 1, may hold values from -6 to 6
- cotangent: bfloat16 [2, 2048, 1536], P('expert', ('groups', 'wide', 'dp')), parts along dimension 1, may hold values from -6 to 6
- frozen_up_weight: bfloat16 [2, 4096, 1536], P('expert', None, 'dp'), may hold values from -0.09375 to 0.09375
- master: float32 [4, 32, 5632], P(('groups', 'expert'), None, ('wide', 'dp')), parts along dimension 0, may hold values from -0.3 to 0.3
- moment_one: float32 [4, 32, 5632], P(('groups', 'expert'), None, ('wide', 'dp')), parts along dimension 0, may hold values from -0.12 to 0.12
- moment_two: float32 [4, 32, 5632], P(('groups', 'expert'), None, ('wide', 'dp')), parts along dimension 0, may hold values from 0.0001 to 0.001
Outputs:
- merged: bfloat16 [4, 4096, 1536], P(('groups', 'expert'), None, 'dp'), parts along dimension 0
- renewed: float32 [4, 32, 5632], P(('groups', 'expert'), None, ('wide', 'dp')), parts along dimension 0
The draws below stay inside these ranges and needn't reach their ends.
There are 2 independent parts, one for each index of `groups`. The reference program is written for one: setup_inputs(seed, part) draws one part's arguments, and reference() takes and returns one part's arrays. A program takes and returns all parts, laid end to end along the dimension named above; an argument that names none is the same for every part. Nothing has to cross between parts.
All inputs are finite; a program needn't handle non-finite values.
Results may differ from the reference program's by a relative error of at most 0.0056.
Values may be sent and summed in bfloat16 or wider, within the bound.
A program may use at most 64 MiB of HBM per device.

```python
import math
import jax
import jax.numpy as jnp

D = 4096
FF = 1536
RANK = 32
EXPERTS = 2
EXPERT_TOKENS = 1024
COLS = 5632


def block_levels(key, dims, pieces, smallest, top_value):
    loudness, own = 1.0, jax.random.fold_in(key, 6)
    for dim, blocks in pieces:
        steps = jnp.exp(jax.random.uniform(jax.random.fold_in(own, dim), (blocks,), jnp.float32, smallest / len(pieces), top_value / len(pieces)))
        loudness = loudness * jnp.repeat(steps, dims[dim] // blocks).reshape([-1 if axis == dim else 1 for axis in range(len(dims))])
    return loudness


def normal_values(stream_key, shape, scale, most, pieces=(), dtype=jnp.bfloat16):
    loudness = block_levels(stream_key, shape, pieces, -0.22, 0.18) if pieces else 1.0
    entries = jax.random.normal(stream_key, shape, jnp.float32) * scale * loudness
    return jnp.minimum(jnp.maximum(entries, -most), most).astype(dtype)


def setup_inputs(seed: int = 0, part: int = 0) -> dict:
    arg_keys = jax.random.split(jax.random.key(seed), 7)
    part_splits = jax.random.split(jax.random.fold_in(arg_keys[6], part), 7)
    tokens = normal_values(part_splits[0], (EXPERTS, EXPERT_TOKENS, D), 1.0, 6.0, ((0, 2), (1, 8)))
    cotangent = normal_values(part_splits[1], (EXPERTS, EXPERT_TOKENS, FF), 1.0, 6.0, ((0, 2), (1, 8)))
    frozen_up_weight = normal_values(arg_keys[2], (EXPERTS, D, FF), D ** -0.5, 0.09375, ((0, 2), (2, 2)))
    master = normal_values(part_splits[3], (EXPERTS, RANK, COLS), 0.05, 0.3, ((0, 2), (2, 8)), jnp.float32)
    moment_one = normal_values(part_splits[4], (EXPERTS, RANK, COLS), 0.02, 0.12, ((0, 2), (2, 8)), jnp.float32)
    moment_two = jnp.clip(jnp.exp(math.log(0.001) - 2.3025852 * jax.random.uniform(part_splits[5], (EXPERTS, RANK, COLS), jnp.float32) ** block_levels(part_splits[5], (EXPERTS, RANK, COLS), ((0, 2), (2, 8)), -0.2, 0.2)), 0.0001, 0.001)
    return {"tokens": tokens, "cotangent": cotangent, "frozen_up_weight": frozen_up_weight, "master": master, "moment_one": moment_one, "moment_two": moment_two}


beta_one = 0.9
beta_two = 0.95
learn_rate = 0.01
weight_decay = 0.1
step_count = 10
eps_adam = 1e-08
low_rank_scale = 2.0

def reference(tokens, cotangent, frozen_up_weight, master, moment_one, moment_two):
    merged_list = []
    renewed_list = []
    for expert_number in range(EXPERTS):
        current = master[expert_number].astype(jnp.bfloat16)
        rows_b = current[:, :D]
        cols_a = current[:, D:]
        hidden = jnp.dot(tokens[expert_number], rows_b.T, preferred_element_type=jnp.float32).astype(jnp.bfloat16)
        back = jnp.dot(cotangent[expert_number], cols_a.T, preferred_element_type=jnp.float32).astype(jnp.bfloat16)
        up_factor = jnp.dot(back.T, tokens[expert_number], preferred_element_type=jnp.float32)
        down_factor = jnp.dot(hidden.T, cotangent[expert_number], preferred_element_type=jnp.float32)
        adapter_gradient = jnp.concatenate([up_factor, down_factor], axis=1) * (low_rank_scale / EXPERT_TOKENS)
        first_new = beta_one * moment_one[expert_number] + (1.0 - beta_one) * adapter_gradient
        second_new = beta_two * moment_two[expert_number] + (1.0 - beta_two) * adapter_gradient * adapter_gradient
        step_size = first_new / (1.0 - beta_one ** step_count) / (jnp.sqrt(second_new / (1.0 - beta_two ** step_count)) + eps_adam)
        renewed = master[expert_number] - learn_rate * (step_size + weight_decay * master[expert_number])
        factors = renewed.astype(jnp.bfloat16)
        factor_product = jnp.dot(factors[:, :D].T, factors[:, D:], preferred_element_type=jnp.float32)
        merged = (frozen_up_weight[expert_number].astype(jnp.float32) + low_rank_scale * factor_product).astype(jnp.bfloat16)
        merged_list.append(merged)
        renewed_list.append(renewed)
    return (jnp.stack(merged_list), jnp.stack(renewed_list))
```

```python
import functools

import jax
import jax.numpy as jnp
from jax import lax
from jax.experimental import pallas as pl
from jax.experimental.pallas import tpu as pltpu
from jax.sharding import PartitionSpec as P

beta_one = 0.9
beta_two = 0.95
learn_rate = 0.01
weight_decay = 0.1
step_count = 10
eps_adam = 1e-08
low_rank_scale = 2.0

MESH = pl.DeviceIdType.MESH
NT = (((1,), (1,)), ((), ()))
TN = (((0,), (0,)), ((), ()))


def adam(master, moment_one, moment_two, gradient):
    first_new = beta_one * moment_one + (1.0 - beta_one) * gradient
    second_new = beta_two * moment_two + (1.0 - beta_two) * gradient * gradient
    step_size = (
        first_new
        / (1.0 - beta_one**step_count)
        / (jnp.sqrt(second_new / (1.0 - beta_two**step_count)) + eps_adam)
    )
    return master - learn_rate * (step_size + weight_decay * master)


def update_kernel(
    nz, scale, tok, cot, mas, mom1, mom2, ren, out_b, out_a,
    both, frame, gat, fac, snd_x, rcv_x, own, snd_z, rcv_z, allf,
    in_sem, g_send, g_recv, x_send, x_recv, z_send, z_recv, f_send, f_recv,
):
    width = tok.shape[2]
    hidden_units = cot.shape[2]
    rank, block = mas.shape[1], mas.shape[2]
    lanes = gat.shape[3]
    main = lanes - 128
    pair = 2 * block
    shift = lanes - block
    z = lax.axis_index("wide")
    x = lax.axis_index("dp")
    xo = 1 - x

    def z_at(distance):
        return lax.rem(z + distance, nz)

    in_tok = pltpu.make_async_copy(tok.at[0], both.at[:, pl.ds(0, width)], in_sem.at[0])
    in_cot = pltpu.make_async_copy(cot.at[0], both.at[:, pl.ds(width, hidden_units)], in_sem.at[1])
    in_tok.start()
    in_cot.start()

    barrier = pltpu.get_barrier_semaphore()
    for d in range(1, nz):
        pl.semaphore_signal(barrier, inc=1, device_id={"wide": z_at(d)}, device_id_type=MESH)
    pl.semaphore_signal(barrier, inc=1, device_id={"dp": xo}, device_id_type=MESH)

    def framed(ref):
        frame[:, main:] = jnp.zeros((rank, 128), jnp.float32)
        frame[:, :block] = ref[0]
        return pltpu.roll(frame[...], x * shift, 1)

    master = framed(mas)
    gat[x, z] = master.astype(jnp.bfloat16)
    pl.semaphore_wait(barrier, nz)

    def share(buf, send, recv):
        sends = []
        for d in range(1, nz):
            sends.append(pltpu.make_async_remote_copy(
                buf.at[x, z], buf.at[x, z], send.at[d - 1], recv.at[x, z],
                device_id={"wide": z_at(d)}, device_id_type=MESH))
        sends.append(pltpu.make_async_remote_copy(
            buf.at[x, z], buf.at[x, z], send.at[nz - 1], recv.at[x, z],
            device_id={"dp": xo}, device_id_type=MESH))
        for copy in sends:
            copy.start()
        return sends

    def arrived(buf, recv, column, row):
        pltpu.make_async_remote_copy(
            buf.at[column, row], buf.at[column, row], recv.at[column, row], recv.at[column, row],
            device_id={"dp": xo}, device_id_type=MESH).wait_recv()

    def forward(buf, send, recv, d):
        row = z_at(nz - d)
        arrived(buf, recv, x, row)
        copy = pltpu.make_async_remote_copy(
            buf.at[x, row], buf.at[x, row], send.at[nz - 1 + d], recv.at[x, row],
            device_id={"dp": xo}, device_id_type=MESH)
        copy.start()
        return copy

    def start_of(row, column):
        return row * pair + column * main_step

    main_step = block - shift

    def is_b(row, column):
        begin = start_of(row, column)
        return begin < width, begin + main < width

    sends = share(gat, g_send, g_recv)
    in_tok.wait()
    in_cot.wait()

    hidden = jnp.zeros((rank, both.shape[0]), jnp.float32)
    back = jnp.zeros((rank, both.shape[0]), jnp.float32)

    def project(row, column, hidden, back):
        begin = start_of(row, column)
        b_main, b_last = is_b(row, column)
        part = lax.dot_general(
            gat[column, row, :, :main], both[:, pl.ds(pl.multiple_of(begin, 128), main)],
            NT, preferred_element_type=jnp.float32)
        last = lax.dot_general(
            gat[column, row, :, main:], both[:, pl.ds(pl.multiple_of(begin + main, 128), 128)],
            NT, preferred_element_type=jnp.float32)
        hidden = hidden + jnp.where(b_main, part, 0.0) + jnp.where(b_last, last, 0.0)
        back = back + jnp.where(b_main, 0.0, part) + jnp.where(b_last, 0.0, last)
        return hidden, back

    for d in range(nz):
        if d:
            sends.append(forward(gat, g_send, g_recv, d))
        hidden, back = project(z_at(nz - d), x, hidden, back)
    for d in range(nz):
        row = z_at(nz - d)
        arrived(gat, g_recv, xo, row)
        hidden, back = project(row, xo, hidden, back)
    for copy in sends:
        copy.wait_send()
    hidden = hidden.astype(jnp.bfloat16).astype(jnp.float32)
    back = back.astype(jnp.bfloat16).astype(jnp.float32)

    def gradient(row, column):
        begin = start_of(row, column)
        b_main, b_last = is_b(row, column)
        part = jnp.dot(
            jnp.where(b_main, back, hidden).astype(jnp.bfloat16),
            both[:, pl.ds(pl.multiple_of(begin, 128), main)], preferred_element_type=jnp.float32)
        last = jnp.dot(
            jnp.where(b_last, back, hidden).astype(jnp.bfloat16),
            both[:, pl.ds(pl.multiple_of(begin + main, 128), 128)], preferred_element_type=jnp.float32)
        return part, last

    x_copies = []
    for i in range(nz):
        row = z_at(i + 1)
        part, last = gradient(row, xo)
        snd_x[row, :, :main] = part.astype(jnp.bfloat16)
        snd_x[row, :, main:] = last.astype(jnp.bfloat16)
        copy = pltpu.make_async_remote_copy(
            snd_x.at[row], rcv_x.at[row], x_send.at[i], x_recv.at[row],
            device_id={"dp": xo}, device_id_type=MESH)
        copy.start()
        x_copies.append(copy)
    for i in range(nz):
        row = z_at(i + 1)
        part, last = gradient(row, x)
        own[row, :, :main] = part
        own[row, :, main:] = last

    moment_one = framed(mom1)
    moment_two = framed(mom2)

    z_copies = []
    for i in range(nz - 1):
        row = z_at(i + 1)
        x_copies[i].wait_recv()
        snd_z[i] = (own[row] + rcv_x[row].astype(jnp.float32)).astype(jnp.bfloat16)
        copy = pltpu.make_async_remote_copy(
            snd_z.at[i], rcv_z.at[z], z_send.at[i], z_recv.at[z],
            device_id={"wide": row}, device_id_type=MESH)
        copy.start()
        z_copies.append(copy)
    x_copies[nz - 1].wait_recv()
    total = own[z] + rcv_x[z].astype(jnp.float32)
    for d in range(1, nz):
        row = z_at(nz - d)
        pltpu.make_async_remote_copy(
            snd_z.at[d - 1], rcv_z.at[row], z_send.at[d - 1], z_recv.at[row],
            device_id={"wide": row}, device_id_type=MESH).wait_recv()
        total = total + rcv_z[row].astype(jnp.float32)

    renewed = adam(master, moment_one, moment_two, total * scale)
    lane = lax.broadcasted_iota(jnp.int32, (rank, lanes), 1)
    first = x * shift
    valid = (lane >= first) & (lane < first + block)
    fac[x, z] = jnp.where(valid, renewed, 0.0).astype(jnp.bfloat16)
    sends = share(fac, f_send, f_recv)
    frame[...] = pltpu.roll(renewed, lanes - x * shift, 1)
    ren[0] = frame[:, :block]

    for copy in x_copies + z_copies:
        copy.wait_send()
    for d in range(1, nz):
        sends.append(forward(fac, f_send, f_recv, d))
    for d in range(nz):
        arrived(fac, f_recv, xo, z_at(nz - d))
    for row in range(nz):
        base = row * pair
        allf[:, base:base + main] = fac[0, row, :, :main]
        joined = fac[0, row, :, main:].astype(jnp.float32) + fac[1, row, :, :128].astype(jnp.float32)
        allf[:, base + main:base + lanes] = joined.astype(jnp.bfloat16)
        allf[:, base + lanes:base + pair] = fac[1, row, :, 128:]
    slice_width = out_a.shape[1]
    out_b[...] = allf[:, :width]
    mine = allf[:, pl.ds(pl.multiple_of(width + x * slice_width, 128), slice_width)]
    out_a[...] = (mine.astype(jnp.float32) * low_rank_scale).astype(jnp.bfloat16)
    for copy in sends:
        copy.wait_send()


def merge_kernel(weight, new_b, new_a, merged):
    product = lax.dot_general(new_b[...], new_a[...], TN, preferred_element_type=jnp.float32)
    merged[0] = (weight[0].astype(jnp.float32) + product).astype(jnp.bfloat16)


def fused_shards(nz, tokens, cotangent, frozen_up_weight, master, moment_one, moment_two):
    rows, width = tokens.shape[1:]
    hidden_units = cotangent.shape[2]
    rank, block = master.shape[1:]
    slice_width = frozen_up_weight.shape[2]
    lanes = block + 64
    bf16, f32 = jnp.bfloat16, jnp.float32
    vmem = pl.BlockSpec(memory_space=pltpu.VMEM)
    anywhere = pl.BlockSpec(memory_space=pl.ANY)
    dma = pltpu.SemaphoreType.DMA
    scale = low_rank_scale / (rows * nz * 2)
    renewed, new_b, new_a = pl.pallas_call(
        functools.partial(update_kernel, nz, scale),
        out_shape=(
            jax.ShapeDtypeStruct(master.shape, f32),
            jax.ShapeDtypeStruct((rank, width), bf16),
            jax.ShapeDtypeStruct((rank, slice_width), bf16),
        ),
        in_specs=[anywhere, anywhere, vmem, vmem, vmem],
        out_specs=(vmem, vmem, vmem),
        scratch_shapes=[
            pltpu.VMEM((rows, width + hidden_units), bf16),
            pltpu.VMEM((rank, lanes), f32),
            pltpu.VMEM((2, nz, rank, lanes), bf16),
            pltpu.VMEM((2, nz, rank, lanes), bf16),
            pltpu.VMEM((nz, rank, lanes), bf16),
            pltpu.VMEM((nz, rank, lanes), bf16),
            pltpu.VMEM((nz, rank, lanes), f32),
            pltpu.VMEM((nz - 1, rank, lanes), bf16),
            pltpu.VMEM((nz, rank, lanes), bf16),
            pltpu.VMEM((rank, width + hidden_units), bf16),
            dma((2,)),
            dma((2 * nz - 1,)),
            dma((2, nz)),
            dma((nz,)),
            dma((nz,)),
            dma((nz - 1,)),
            dma((nz,)),
            dma((2 * nz - 1,)),
            dma((2, nz)),
        ],
        compiler_params=pltpu.CompilerParams(
            collective_id=0, has_side_effects=True, vmem_limit_bytes=12 * 1024 * 1024
        ),
    )(tokens, cotangent, master, moment_one, moment_two)
    step = 512
    merged = pl.pallas_call(
        merge_kernel,
        grid=(width // step,),
        out_shape=jax.ShapeDtypeStruct(frozen_up_weight.shape, bf16),
        in_specs=[
            pl.BlockSpec((1, step, slice_width), lambda i: (0, i, 0)),
            pl.BlockSpec((rank, step), lambda i: (0, i)),
            pl.BlockSpec((rank, slice_width), lambda i: (0, 0)),
        ],
        out_specs=pl.BlockSpec((1, step, slice_width), lambda i: (0, i, 0)),
        compiler_params=pltpu.CompilerParams(vmem_limit_bytes=16 * 1024 * 1024),
    )(frozen_up_weight, new_b, new_a)
    return merged, renewed


def shards(tokens, cotangent, frozen_up_weight, master, moment_one, moment_two):
    wide_count = lax.axis_size("wide")
    data_count = lax.axis_size("dp")
    width = tokens.shape[2]
    inputs = tokens[0]
    upstream = cotangent[0]
    current = master[0].astype(jnp.bfloat16)
    gathered = lax.all_gather(current, ("wide", "dp"), axis=1, tiled=True)
    rows_b = gathered[:, :width]
    cols_a = gathered[:, width:]
    hidden = jnp.dot(inputs, rows_b.T, preferred_element_type=jnp.float32).astype(jnp.bfloat16)
    back = jnp.dot(upstream, cols_a.T, preferred_element_type=jnp.float32).astype(jnp.bfloat16)
    up_factor = jnp.dot(back.T, inputs, preferred_element_type=jnp.float32)
    down_factor = jnp.dot(hidden.T, upstream, preferred_element_type=jnp.float32)
    partial_value = jnp.concatenate([up_factor, down_factor], axis=1)
    reduced_total = lax.psum_scatter(partial_value, ("wide", "dp"), scatter_dimension=1, tiled=True)
    gathered_rows = inputs.shape[0] * wide_count * data_count
    adapter_gradient = reduced_total * (low_rank_scale / gathered_rows)
    renewed = adam(master[0], moment_one[0], moment_two[0], adapter_gradient)
    factors = renewed.astype(jnp.bfloat16)
    all_factors = lax.all_gather(factors, ("wide", "dp"), axis=1, tiled=True)
    slice_width = frozen_up_weight.shape[2]
    data_index = lax.axis_index("dp")
    new_b = all_factors[:, :width]
    new_a = lax.dynamic_slice_in_dim(all_factors, width + data_index * slice_width, slice_width, 1)
    factor_product = jnp.dot(new_b.T, new_a, preferred_element_type=jnp.float32)
    merged = (frozen_up_weight[0].astype(jnp.float32) + low_rank_scale * factor_product).astype(
        jnp.bfloat16
    )
    return (merged[None], renewed[None])


def frame_fits(nz, nx, width, block, slice_width):
    if nx != 2 or nz < 2 or nz > 8 or block % 128 != 64 or block < 192 or width % 512 or slice_width % 128:
        return False
    for row in range(nz):
        for column in range(2):
            begin = row * 2 * block + column * (block - 64)
            if begin < width < begin + block - 64:
                return False
    return True


def solution(mesh):
    nz, nx = mesh.shape["wide"], mesh.shape["dp"]

    def per_device(tokens, cotangent, frozen_up_weight, master, moment_one, moment_two):
        args = (tokens, cotangent, frozen_up_weight, master, moment_one, moment_two)
        if frame_fits(nz, nx, tokens.shape[2], master.shape[2], frozen_up_weight.shape[2]):
            return fused_shards(nz, *args)
        return shards(*args)

    in_specs = (
        P("expert", ("groups", "wide", "dp"), None),
        P("expert", ("groups", "wide", "dp"), None),
        P("expert", None, "dp"),
        P(("groups", "expert"), None, ("wide", "dp")),
        P(("groups", "expert"), None, ("wide", "dp")),
        P(("groups", "expert"), None, ("wide", "dp")),
    )
    out_specs = (P(("groups", "expert"), None, "dp"), P(("groups", "expert"), None, ("wide", "dp")))
    return jax.shard_map(per_device, mesh=mesh, in_specs=in_specs, out_specs=out_specs, check_vma=False)
```

```python
import functools

import jax
import jax.numpy as jnp
from jax import lax
from jax.experimental import pallas as pl
from jax.experimental.pallas import tpu as pltpu
from jax.sharding import PartitionSpec as P

beta_one = 0.9
beta_two = 0.95
learn_rate = 0.01
weight_decay = 0.1
step_count = 10
eps_adam = 1e-08
low_rank_scale = 2.0

MESH = pl.DeviceIdType.MESH
NT = (((1,), (1,)), ((), ()))
TN = (((0,), (0,)), ((), ()))


def adam(master, moment_one, moment_two, gradient):
    first_new = beta_one * moment_one + (1.0 - beta_one) * gradient
    second_new = beta_two * moment_two + (1.0 - beta_two) * gradient * gradient
    step_size = (
        first_new
        / (1.0 - beta_one**step_count)
        / (jnp.sqrt(second_new / (1.0 - beta_two**step_count)) + eps_adam)
    )
    return master - learn_rate * (step_size + weight_decay * master)


def update_kernel(
    nz, scale, tok, cot, mas_hbm, mom1_hbm, mom2_hbm, weight, ren, out_b, out_a, held,
    both, mas, mom1, mom2, frame, gat, fac, snd_x, rcv_x, own, snd_z, rcv_z, allf,
    in_sem, g_send, g_recv, x_send, x_recv, z_send, z_recv, f_send, f_recv,
):
    width = tok.shape[2]
    hidden_units = cot.shape[2]
    rank, block = mas.shape[1], mas.shape[2]
    lanes = gat.shape[3]
    main = lanes - 128
    pair = 2 * block
    shift = lanes - block
    z = lax.axis_index("wide")
    x = lax.axis_index("dp")
    xo = 1 - x

    def z_at(distance):
        return lax.rem(z + distance, nz)

    in_tok = pltpu.make_async_copy(tok.at[0], both.at[:, pl.ds(0, width)], in_sem.at[0])
    in_cot = pltpu.make_async_copy(cot.at[0], both.at[:, pl.ds(width, hidden_units)], in_sem.at[1])
    in_mas = pltpu.make_async_copy(mas_hbm, mas, in_sem.at[2])
    in_mom1 = pltpu.make_async_copy(mom1_hbm, mom1, in_sem.at[3])
    in_mom2 = pltpu.make_async_copy(mom2_hbm, mom2, in_sem.at[4])
    in_weight = pltpu.make_async_copy(weight, held, in_sem.at[5])
    for copy in (in_mas, in_tok, in_cot, in_mom1, in_mom2, in_weight):
        copy.start()

    barrier = pltpu.get_barrier_semaphore()
    for d in range(1, nz):
        pl.semaphore_signal(barrier, inc=1, device_id={"wide": z_at(d)}, device_id_type=MESH)
    pl.semaphore_signal(barrier, inc=1, device_id={"dp": xo}, device_id_type=MESH)

    def framed(ref):
        frame[:, main:] = jnp.zeros((rank, 128), jnp.float32)
        frame[:, :block] = ref[0]
        return pltpu.roll(frame[...], x * shift, 1)

    in_mas.wait()
    master = framed(mas)
    gat[x, z] = master.astype(jnp.bfloat16)
    pl.semaphore_wait(barrier, nz)

    def share(buf, send, recv):
        sends = []
        for d in range(1, nz):
            sends.append(pltpu.make_async_remote_copy(
                buf.at[x, z], buf.at[x, z], send.at[d - 1], recv.at[x, z],
                device_id={"wide": z_at(d)}, device_id_type=MESH))
        sends.append(pltpu.make_async_remote_copy(
            buf.at[x, z], buf.at[x, z], send.at[nz - 1], recv.at[x, z],
            device_id={"dp": xo}, device_id_type=MESH))
        for copy in sends:
            copy.start()
        return sends

    def arrived(buf, recv, column, row):
        pltpu.make_async_remote_copy(
            buf.at[column, row], buf.at[column, row], recv.at[column, row], recv.at[column, row],
            device_id={"dp": xo}, device_id_type=MESH).wait_recv()

    def forward(buf, send, recv, d):
        row = z_at(nz - d)
        arrived(buf, recv, x, row)
        copy = pltpu.make_async_remote_copy(
            buf.at[x, row], buf.at[x, row], send.at[nz - 1 + d], recv.at[x, row],
            device_id={"dp": xo}, device_id_type=MESH)
        copy.start()
        return copy

    def start_of(row, column):
        return row * pair + column * main_step

    main_step = block - shift

    def is_b(row, column):
        begin = start_of(row, column)
        return begin < width, begin + main < width

    sends = share(gat, g_send, g_recv)
    in_tok.wait()
    in_cot.wait()

    hidden = jnp.zeros((rank, both.shape[0]), jnp.float32)
    back = jnp.zeros((rank, both.shape[0]), jnp.float32)

    def project(row, column, hidden, back):
        begin = start_of(row, column)
        b_main, b_last = is_b(row, column)
        part = lax.dot_general(
            gat[column, row, :, :main], both[:, pl.ds(pl.multiple_of(begin, 128), main)],
            NT, preferred_element_type=jnp.float32)
        last = lax.dot_general(
            gat[column, row, :, main:], both[:, pl.ds(pl.multiple_of(begin + main, 128), 128)],
            NT, preferred_element_type=jnp.float32)
        hidden = hidden + jnp.where(b_main, part, 0.0) + jnp.where(b_last, last, 0.0)
        back = back + jnp.where(b_main, 0.0, part) + jnp.where(b_last, 0.0, last)
        return hidden, back

    for d in range(nz):
        if d:
            sends.append(forward(gat, g_send, g_recv, d))
        hidden, back = project(z_at(nz - d), x, hidden, back)
    for d in range(nz):
        row = z_at(nz - d)
        arrived(gat, g_recv, xo, row)
        hidden, back = project(row, xo, hidden, back)
    for copy in sends:
        copy.wait_send()
    hidden = hidden.astype(jnp.bfloat16).astype(jnp.float32)
    back = back.astype(jnp.bfloat16).astype(jnp.float32)

    def gradient(row, column):
        begin = start_of(row, column)
        b_main, b_last = is_b(row, column)
        part = jnp.dot(
            jnp.where(b_main, back, hidden).astype(jnp.bfloat16),
            both[:, pl.ds(pl.multiple_of(begin, 128), main)], preferred_element_type=jnp.float32)
        last = jnp.dot(
            jnp.where(b_last, back, hidden).astype(jnp.bfloat16),
            both[:, pl.ds(pl.multiple_of(begin + main, 128), 128)], preferred_element_type=jnp.float32)
        return part, last

    x_copies = []
    for i in range(nz):
        row = z_at(i + 1)
        part, last = gradient(row, xo)
        snd_x[row, :, :main] = part.astype(jnp.bfloat16)
        snd_x[row, :, main:] = last.astype(jnp.bfloat16)
        copy = pltpu.make_async_remote_copy(
            snd_x.at[row], rcv_x.at[row], x_send.at[i], x_recv.at[row],
            device_id={"dp": xo}, device_id_type=MESH)
        copy.start()
        x_copies.append(copy)
    for i in range(nz):
        row = z_at(i + 1)
        part, last = gradient(row, x)
        own[row, :, :main] = part
        own[row, :, main:] = last

    in_mom1.wait()
    in_mom2.wait()
    moment_one = framed(mom1)
    moment_two = framed(mom2)

    z_copies = []
    for i in range(nz - 1):
        row = z_at(i + 1)
        x_copies[i].wait_recv()
        snd_z[i] = (own[row] + rcv_x[row].astype(jnp.float32)).astype(jnp.bfloat16)
        copy = pltpu.make_async_remote_copy(
            snd_z.at[i], rcv_z.at[z], z_send.at[i], z_recv.at[z],
            device_id={"wide": row}, device_id_type=MESH)
        copy.start()
        z_copies.append(copy)
    x_copies[nz - 1].wait_recv()
    total = own[z] + rcv_x[z].astype(jnp.float32)
    for d in range(1, nz):
        row = z_at(nz - d)
        pltpu.make_async_remote_copy(
            snd_z.at[d - 1], rcv_z.at[row], z_send.at[d - 1], z_recv.at[row],
            device_id={"wide": row}, device_id_type=MESH).wait_recv()
        total = total + rcv_z[row].astype(jnp.float32)

    renewed = adam(master, moment_one, moment_two, total * scale)
    lane = lax.broadcasted_iota(jnp.int32, (rank, lanes), 1)
    first = x * shift
    valid = (lane >= first) & (lane < first + block)
    fac[x, z] = jnp.where(valid, renewed, 0.0).astype(jnp.bfloat16)
    sends = share(fac, f_send, f_recv)
    frame[...] = pltpu.roll(renewed, lanes - x * shift, 1)
    ren[0] = frame[:, :block]

    for copy in x_copies + z_copies:
        copy.wait_send()
    for d in range(1, nz):
        sends.append(forward(fac, f_send, f_recv, d))
    for d in range(nz):
        arrived(fac, f_recv, xo, z_at(nz - d))
    for row in range(nz):
        base = row * pair
        allf[:, base:base + main] = fac[0, row, :, :main]
        joined = fac[0, row, :, main:].astype(jnp.float32) + fac[1, row, :, :128].astype(jnp.float32)
        allf[:, base + main:base + lanes] = joined.astype(jnp.bfloat16)
        allf[:, base + lanes:base + pair] = fac[1, row, :, 128:]
    slice_width = out_a.shape[1]
    out_b[...] = allf[:, :width]
    mine = allf[:, pl.ds(pl.multiple_of(width + x * slice_width, 128), slice_width)]
    out_a[...] = (mine.astype(jnp.float32) * low_rank_scale).astype(jnp.bfloat16)
    for copy in sends:
        copy.wait_send()
    in_weight.wait()


def merge_kernel(step, weight, new_b, new_a, ren, merged, ren_out, staged, sem):
    ren_copy = pltpu.make_async_copy(ren, ren_out, sem.at[0])
    ren_copy.start()
    copies = []
    for i in range(staged.shape[0] // step):
        part = pl.ds(i * step, step)
        product = lax.dot_general(new_b[:, part], new_a[...], TN, preferred_element_type=jnp.float32)
        staged[part] = (weight[0, part].astype(jnp.float32) + product).astype(jnp.bfloat16)
        copy = pltpu.make_async_copy(staged.at[part], merged.at[0, part], sem.at[i + 1])
        copy.start()
        copies.append(copy)
    for copy in copies + [ren_copy]:
        copy.wait()


def fused_shards(nz, tokens, cotangent, frozen_up_weight, master, moment_one, moment_two):
    rows, width = tokens.shape[1:]
    hidden_units = cotangent.shape[2]
    rank, block = master.shape[1:]
    slice_width = frozen_up_weight.shape[2]
    lanes = block + 64
    bf16, f32 = jnp.bfloat16, jnp.float32
    vmem = pl.BlockSpec(memory_space=pltpu.VMEM)
    hbm = pl.BlockSpec(memory_space=pltpu.HBM)
    dma = pltpu.SemaphoreType.DMA
    scale = low_rank_scale / (rows * nz * 2)
    renewed, new_b, new_a, held = pl.pallas_call(
        functools.partial(update_kernel, nz, scale),
        out_shape=(
            pltpu.VMEM(master.shape, f32),
            pltpu.VMEM((rank, width), bf16),
            pltpu.VMEM((rank, slice_width), bf16),
            pltpu.VMEM(frozen_up_weight.shape, bf16),
        ),
        in_specs=[hbm] * 6,
        out_specs=(vmem,) * 4,
        scratch_shapes=[
            pltpu.VMEM((rows, width + hidden_units), bf16),
            pltpu.VMEM(master.shape, f32),
            pltpu.VMEM(master.shape, f32),
            pltpu.VMEM(master.shape, f32),
            pltpu.VMEM((rank, lanes), f32),
            pltpu.VMEM((2, nz, rank, lanes), bf16),
            pltpu.VMEM((2, nz, rank, lanes), bf16),
            pltpu.VMEM((nz, rank, lanes), bf16),
            pltpu.VMEM((nz, rank, lanes), bf16),
            pltpu.VMEM((nz, rank, lanes), f32),
            pltpu.VMEM((nz - 1, rank, lanes), bf16),
            pltpu.VMEM((nz, rank, lanes), bf16),
            pltpu.VMEM((rank, width + hidden_units), bf16),
            dma((6,)),
            dma((2 * nz - 1,)),
            dma((2, nz)),
            dma((nz,)),
            dma((nz,)),
            dma((nz - 1,)),
            dma((nz,)),
            dma((2 * nz - 1,)),
            dma((2, nz)),
        ],
        compiler_params=pltpu.CompilerParams(
            collective_id=0, has_side_effects=True, vmem_limit_bytes=56 * 1024 * 1024
        ),
    )(tokens, cotangent, master, moment_one, moment_two, frozen_up_weight)
    step = 512
    merged, renewed = pl.pallas_call(
        functools.partial(merge_kernel, step),
        out_shape=(
            jax.ShapeDtypeStruct(frozen_up_weight.shape, bf16),
            jax.ShapeDtypeStruct(master.shape, f32),
        ),
        in_specs=[vmem] * 4,
        out_specs=(hbm, hbm),
        scratch_shapes=[pltpu.VMEM((width, slice_width), bf16), dma((width // step + 1,))],
        compiler_params=pltpu.CompilerParams(vmem_limit_bytes=20 * 1024 * 1024),
    )(held, new_b, new_a, renewed)
    return merged, renewed


def shards(tokens, cotangent, frozen_up_weight, master, moment_one, moment_two):
    wide_count = lax.axis_size("wide")
    data_count = lax.axis_size("dp")
    width = tokens.shape[2]
    inputs = tokens[0]
    upstream = cotangent[0]
    current = master[0].astype(jnp.bfloat16)
    gathered = lax.all_gather(current, ("wide", "dp"), axis=1, tiled=True)
    rows_b = gathered[:, :width]
    cols_a = gathered[:, width:]
    hidden = jnp.dot(inputs, rows_b.T, preferred_element_type=jnp.float32).astype(jnp.bfloat16)
    back = jnp.dot(upstream, cols_a.T, preferred_element_type=jnp.float32).astype(jnp.bfloat16)
    up_factor = jnp.dot(back.T, inputs, preferred_element_type=jnp.float32)
    down_factor = jnp.dot(hidden.T, upstream, preferred_element_type=jnp.float32)
    partial_value = jnp.concatenate([up_factor, down_factor], axis=1)
    reduced_total = lax.psum_scatter(partial_value, ("wide", "dp"), scatter_dimension=1, tiled=True)
    gathered_rows = inputs.shape[0] * wide_count * data_count
    adapter_gradient = reduced_total * (low_rank_scale / gathered_rows)
    renewed = adam(master[0], moment_one[0], moment_two[0], adapter_gradient)
    factors = renewed.astype(jnp.bfloat16)
    all_factors = lax.all_gather(factors, ("wide", "dp"), axis=1, tiled=True)
    slice_width = frozen_up_weight.shape[2]
    data_index = lax.axis_index("dp")
    new_b = all_factors[:, :width]
    new_a = lax.dynamic_slice_in_dim(all_factors, width + data_index * slice_width, slice_width, 1)
    factor_product = jnp.dot(new_b.T, new_a, preferred_element_type=jnp.float32)
    merged = (frozen_up_weight[0].astype(jnp.float32) + low_rank_scale * factor_product).astype(
        jnp.bfloat16
    )
    return (merged[None], renewed[None])


def frame_fits(nz, nx, width, block, slice_width):
    if nx != 2 or nz < 2 or nz > 8 or block % 128 != 64 or block < 192 or width % 512 or slice_width % 128:
        return False
    for row in range(nz):
        for column in range(2):
            begin = row * 2 * block + column * (block - 64)
            if begin < width < begin + block - 64:
                return False
    return True


def solution(mesh):
    nz, nx = mesh.shape["wide"], mesh.shape["dp"]

    def per_device(tokens, cotangent, frozen_up_weight, master, moment_one, moment_two):
        args = (tokens, cotangent, frozen_up_weight, master, moment_one, moment_two)
        if frame_fits(nz, nx, tokens.shape[2], master.shape[2], frozen_up_weight.shape[2]):
            return fused_shards(nz, *args)
        return shards(*args)

    in_specs = (
        P("expert", ("groups", "wide", "dp"), None),
        P("expert", ("groups", "wide", "dp"), None),
        P("expert", None, "dp"),
        P(("groups", "expert"), None, ("wide", "dp")),
        P(("groups", "expert"), None, ("wide", "dp")),
        P(("groups", "expert"), None, ("wide", "dp")),
    )
    out_specs = (P(("groups", "expert"), None, "dp"), P(("groups", "expert"), None, ("wide", "dp")))
    return jax.shard_map(per_device, mesh=mesh, in_specs=in_specs, out_specs=out_specs, check_vma=False)
```

```python
import functools

import jax
import jax.numpy as jnp
from jax import lax
from jax.experimental import pallas as pl
from jax.experimental.pallas import tpu as pltpu
from jax.sharding import PartitionSpec as P

beta_one = 0.9
beta_two = 0.95
learn_rate = 0.01
weight_decay = 0.1
step_count = 10
eps_adam = 1e-08
low_rank_scale = 2.0

MESH = pl.DeviceIdType.MESH
DIRECT = 1
NT = (((1,), (1,)), ((), ()))
TN = (((0,), (0,)), ((), ()))


def adam(master, moment_one, moment_two, gradient):
    first_new = beta_one * moment_one + (1.0 - beta_one) * gradient
    second_new = beta_two * moment_two + (1.0 - beta_two) * gradient * gradient
    step_size = (
        first_new
        / (1.0 - beta_one**step_count)
        / (jnp.sqrt(second_new / (1.0 - beta_two**step_count)) + eps_adam)
    )
    return master - learn_rate * (step_size + weight_decay * master)


def update_kernel(
    nz, scale, tok, cot, mas_hbm, mom1_hbm, mom2_hbm, weight, ren, out_b, out_a, held,
    both, mas, mom1, mom2, frame, gat, fac, snd_x, rcv_x, own, snd_z, rcv_z, straight, allf,
    in_sem, g_send, g_recv, x_send, x_recv, z_send, z_recv, f_send, f_recv,
):
    width = tok.shape[2]
    hidden_units = cot.shape[2]
    rank, block = mas.shape[1], mas.shape[2]
    lanes = gat.shape[3]
    main = lanes - 128
    pair = 2 * block
    shift = lanes - block
    z = lax.axis_index("wide")
    x = lax.axis_index("dp")
    xo = 1 - x

    def z_at(distance):
        return lax.rem(z + distance, nz)

    in_tok = pltpu.make_async_copy(tok.at[0], both.at[:, pl.ds(0, width)], in_sem.at[0])
    in_cot = pltpu.make_async_copy(cot.at[0], both.at[:, pl.ds(width, hidden_units)], in_sem.at[1])
    in_mas = pltpu.make_async_copy(mas_hbm, mas, in_sem.at[2])
    in_mom1 = pltpu.make_async_copy(mom1_hbm, mom1, in_sem.at[3])
    in_mom2 = pltpu.make_async_copy(mom2_hbm, mom2, in_sem.at[4])
    in_weight = pltpu.make_async_copy(weight, held, in_sem.at[5])
    for copy in (in_mas, in_tok, in_cot, in_mom1, in_mom2, in_weight):
        copy.start()

    barrier = pltpu.get_barrier_semaphore()
    for d in range(1, nz):
        pl.semaphore_signal(barrier, inc=1, device_id={"wide": z_at(d)}, device_id_type=MESH)
    pl.semaphore_signal(barrier, inc=1, device_id={"dp": xo}, device_id_type=MESH)
    for d in (1, nz - 1):
        pl.semaphore_signal(barrier, inc=1, device_id={"wide": z_at(d), "dp": xo}, device_id_type=MESH)

    def framed(ref):
        frame[:, main:] = jnp.zeros((rank, 128), jnp.float32)
        frame[:, :block] = ref[0]
        return pltpu.roll(frame[...], x * shift, 1)

    in_mas.wait()
    master = framed(mas)
    gat[x, z] = master.astype(jnp.bfloat16)
    pl.semaphore_wait(barrier, nz + 2)

    def share(buf, send, recv):
        targets = [(z_at(d), x) for d in range(2, nz)] + [(z_at(1), x), (z_at(1), xo), (z, xo)]
        sends = []
        for i, (row, column) in enumerate(targets):
            sends.append(pltpu.make_async_remote_copy(
                buf.at[x, z], buf.at[x, z], send.at[i], recv.at[x, z],
                device_id={"wide": row, "dp": column}, device_id_type=MESH))
        for copy in sends:
            copy.start()
        return sends

    def arrived(buf, recv, column, row):
        pltpu.make_async_remote_copy(
            buf.at[column, row], buf.at[column, row], recv.at[column, row], recv.at[column, row],
            device_id={"dp": xo}, device_id_type=MESH).wait_recv()

    def forward(buf, send, recv, d):
        row = z_at(nz - d)
        arrived(buf, recv, x, row)
        copy = pltpu.make_async_remote_copy(
            buf.at[x, row], buf.at[x, row], send.at[nz - 1 + d], recv.at[x, row],
            device_id={"dp": xo}, device_id_type=MESH)
        copy.start()
        return copy

    def start_of(row, column):
        return row * pair + column * main_step

    main_step = block - shift

    def is_b(row, column):
        begin = start_of(row, column)
        return begin < width, begin + main < width

    sends = share(gat, g_send, g_recv)
    in_tok.wait()
    in_cot.wait()

    hidden = jnp.zeros((rank, both.shape[0]), jnp.float32)
    back = jnp.zeros((rank, both.shape[0]), jnp.float32)

    def project(row, column, hidden, back):
        begin = start_of(row, column)
        b_main, b_last = is_b(row, column)
        part = lax.dot_general(
            gat[column, row, :, :main], both[:, pl.ds(pl.multiple_of(begin, 128), main)],
            NT, preferred_element_type=jnp.float32)
        last = lax.dot_general(
            gat[column, row, :, main:], both[:, pl.ds(pl.multiple_of(begin + main, 128), 128)],
            NT, preferred_element_type=jnp.float32)
        hidden = hidden + jnp.where(b_main, part, 0.0) + jnp.where(b_last, last, 0.0)
        back = back + jnp.where(b_main, 0.0, part) + jnp.where(b_last, 0.0, last)
        return hidden, back

    hidden, back = project(z, x, hidden, back)
    for d in range(2, nz):
        sends.append(forward(gat, g_send, g_recv, d))
        hidden, back = project(z_at(nz - d), x, hidden, back)
    arrived(gat, g_recv, x, z_at(nz - 1))
    hidden, back = project(z_at(nz - 1), x, hidden, back)
    for d in range(nz):
        row = z_at(nz - d)
        arrived(gat, g_recv, xo, row)
        hidden, back = project(row, xo, hidden, back)
    hidden = hidden.astype(jnp.bfloat16).astype(jnp.float32)
    back = back.astype(jnp.bfloat16).astype(jnp.float32)

    def gradient(row, column):
        begin = start_of(row, column)
        b_main, b_last = is_b(row, column)
        part = jnp.dot(
            jnp.where(b_main, back, hidden).astype(jnp.bfloat16),
            both[:, pl.ds(pl.multiple_of(begin, 128), main)], preferred_element_type=jnp.float32)
        last = jnp.dot(
            jnp.where(b_last, back, hidden).astype(jnp.bfloat16),
            both[:, pl.ds(pl.multiple_of(begin + main, 128), 128)], preferred_element_type=jnp.float32)
        return part, last

    direct = DIRECT % nz
    order = [d for d in range(nz - 1, 0, -1) if d != direct] + [direct, 0]
    x_copies = []
    for i, d in enumerate(order):
        row = z_at(d)
        target = {"wide": row, "dp": xo} if d == direct else {"dp": xo}
        part, last = gradient(row, xo)
        snd_x[i, :, :main] = part.astype(jnp.bfloat16)
        snd_x[i, :, main:] = last.astype(jnp.bfloat16)
        landing = straight if d == direct else rcv_x.at[i]
        copy = pltpu.make_async_remote_copy(
            snd_x.at[i], landing, x_send.at[i], x_recv.at[i],
            device_id=target, device_id_type=MESH)
        copy.start()
        x_copies.append(copy)
    for i, d in enumerate(order):
        part, last = gradient(z_at(d), x)
        own[i, :, :main] = part
        own[i, :, main:] = last

    in_mom1.wait()
    in_mom2.wait()
    moment_one = framed(mom1)
    moment_two = framed(mom2)

    z_copies = []
    for i in (nz - 2, *range(nz - 2)):
        row = z_at(order[i])
        part = own[i]
        if order[i] != direct:
            x_copies[i].wait_recv()
            part = part + rcv_x[i].astype(jnp.float32)
        snd_z[i] = part.astype(jnp.bfloat16)
        copy = pltpu.make_async_remote_copy(
            snd_z.at[i], rcv_z.at[z], z_send.at[i], z_recv.at[z],
            device_id={"wide": row}, device_id_type=MESH)
        copy.start()
        z_copies.append(copy)
    x_copies[nz - 1].wait_recv()
    x_copies[nz - 2].wait_recv()
    total = own[nz - 1] + rcv_x[nz - 1].astype(jnp.float32) + straight[...].astype(jnp.float32)
    for d in range(1, nz):
        row = z_at(nz - d)
        pltpu.make_async_remote_copy(
            snd_z.at[d - 1], rcv_z.at[row], z_send.at[d - 1], z_recv.at[row],
            device_id={"wide": row}, device_id_type=MESH).wait_recv()
        total = total + rcv_z[row].astype(jnp.float32)

    renewed = adam(master, moment_one, moment_two, total * scale)
    lane = lax.broadcasted_iota(jnp.int32, (rank, lanes), 1)
    first = x * shift
    valid = (lane >= first) & (lane < first + block)
    fac[x, z] = jnp.where(valid, renewed, 0.0).astype(jnp.bfloat16)
    sends += share(fac, f_send, f_recv)
    frame[...] = pltpu.roll(renewed, lanes - x * shift, 1)
    ren[0] = frame[:, :block]

    for d in range(2, nz):
        sends.append(forward(fac, f_send, f_recv, d))
    arrived(fac, f_recv, x, z_at(nz - 1))
    for d in range(nz):
        arrived(fac, f_recv, xo, z_at(nz - d))
    for row in range(nz):
        base = row * pair
        allf[:, base:base + main] = fac[0, row, :, :main]
        joined = fac[0, row, :, main:].astype(jnp.float32) + fac[1, row, :, :128].astype(jnp.float32)
        allf[:, base + main:base + lanes] = joined.astype(jnp.bfloat16)
        allf[:, base + lanes:base + pair] = fac[1, row, :, 128:]
    slice_width = out_a.shape[1]
    out_b[...] = allf[:, :width]
    mine = allf[:, pl.ds(pl.multiple_of(width + x * slice_width, 128), slice_width)]
    out_a[...] = (mine.astype(jnp.float32) * low_rank_scale).astype(jnp.bfloat16)
    for copy in sends + x_copies + z_copies:
        copy.wait_send()
    in_weight.wait()


def merge_kernel(step, weight, new_b, new_a, ren, merged, ren_out, staged, sem):
    ren_copy = pltpu.make_async_copy(ren, ren_out, sem.at[0])
    ren_copy.start()
    copies = []
    for i in range(staged.shape[0] // step):
        part = pl.ds(i * step, step)
        product = lax.dot_general(new_b[:, part], new_a[...], TN, preferred_element_type=jnp.float32)
        staged[part] = (weight[0, part].astype(jnp.float32) + product).astype(jnp.bfloat16)
        copy = pltpu.make_async_copy(staged.at[part], merged.at[0, part], sem.at[i + 1])
        copy.start()
        copies.append(copy)
    for copy in copies + [ren_copy]:
        copy.wait()


def fused_shards(nz, tokens, cotangent, frozen_up_weight, master, moment_one, moment_two):
    rows, width = tokens.shape[1:]
    hidden_units = cotangent.shape[2]
    rank, block = master.shape[1:]
    slice_width = frozen_up_weight.shape[2]
    lanes = block + 64
    bf16, f32 = jnp.bfloat16, jnp.float32
    vmem = pl.BlockSpec(memory_space=pltpu.VMEM)
    hbm = pl.BlockSpec(memory_space=pltpu.HBM)
    dma = pltpu.SemaphoreType.DMA
    scale = low_rank_scale / (rows * nz * 2)
    renewed, new_b, new_a, held = pl.pallas_call(
        functools.partial(update_kernel, nz, scale),
        out_shape=(
            pltpu.VMEM(master.shape, f32),
            pltpu.VMEM((rank, width), bf16),
            pltpu.VMEM((rank, slice_width), bf16),
            pltpu.VMEM(frozen_up_weight.shape, bf16),
        ),
        in_specs=[hbm] * 6,
        out_specs=(vmem,) * 4,
        scratch_shapes=[
            pltpu.VMEM((rows, width + hidden_units), bf16),
            pltpu.VMEM(master.shape, f32),
            pltpu.VMEM(master.shape, f32),
            pltpu.VMEM(master.shape, f32),
            pltpu.VMEM((rank, lanes), f32),
            pltpu.VMEM((2, nz, rank, lanes), bf16),
            pltpu.VMEM((2, nz, rank, lanes), bf16),
            pltpu.VMEM((nz, rank, lanes), bf16),
            pltpu.VMEM((nz, rank, lanes), bf16),
            pltpu.VMEM((nz, rank, lanes), f32),
            pltpu.VMEM((nz - 1, rank, lanes), bf16),
            pltpu.VMEM((nz, rank, lanes), bf16),
            pltpu.VMEM((rank, lanes), bf16),
            pltpu.VMEM((rank, width + hidden_units), bf16),
            dma((6,)),
            dma((2 * nz,)),
            dma((2, nz)),
            dma((nz,)),
            dma((nz,)),
            dma((nz - 1,)),
            dma((nz,)),
            dma((2 * nz,)),
            dma((2, nz)),
        ],
        compiler_params=pltpu.CompilerParams(
            collective_id=0, has_side_effects=True, vmem_limit_bytes=56 * 1024 * 1024
        ),
    )(tokens, cotangent, master, moment_one, moment_two, frozen_up_weight)
    step = 512
    merged, renewed = pl.pallas_call(
        functools.partial(merge_kernel, step),
        out_shape=(
            jax.ShapeDtypeStruct(frozen_up_weight.shape, bf16),
            jax.ShapeDtypeStruct(master.shape, f32),
        ),
        in_specs=[vmem] * 4,
        out_specs=(hbm, hbm),
        scratch_shapes=[pltpu.VMEM((width, slice_width), bf16), dma((width // step + 1,))],
        compiler_params=pltpu.CompilerParams(vmem_limit_bytes=20 * 1024 * 1024),
    )(held, new_b, new_a, renewed)
    return merged, renewed


def shards(tokens, cotangent, frozen_up_weight, master, moment_one, moment_two):
    wide_count = lax.axis_size("wide")
    data_count = lax.axis_size("dp")
    width = tokens.shape[2]
    inputs = tokens[0]
    upstream = cotangent[0]
    current = master[0].astype(jnp.bfloat16)
    gathered = lax.all_gather(current, ("wide", "dp"), axis=1, tiled=True)
    rows_b = gathered[:, :width]
    cols_a = gathered[:, width:]
    hidden = jnp.dot(inputs, rows_b.T, preferred_element_type=jnp.float32).astype(jnp.bfloat16)
    back = jnp.dot(upstream, cols_a.T, preferred_element_type=jnp.float32).astype(jnp.bfloat16)
    up_factor = jnp.dot(back.T, inputs, preferred_element_type=jnp.float32)
    down_factor = jnp.dot(hidden.T, upstream, preferred_element_type=jnp.float32)
    partial_value = jnp.concatenate([up_factor, down_factor], axis=1)
    reduced_total = lax.psum_scatter(partial_value, ("wide", "dp"), scatter_dimension=1, tiled=True)
    gathered_rows = inputs.shape[0] * wide_count * data_count
    adapter_gradient = reduced_total * (low_rank_scale / gathered_rows)
    renewed = adam(master[0], moment_one[0], moment_two[0], adapter_gradient)
    factors = renewed.astype(jnp.bfloat16)
    all_factors = lax.all_gather(factors, ("wide", "dp"), axis=1, tiled=True)
    slice_width = frozen_up_weight.shape[2]
    data_index = lax.axis_index("dp")
    new_b = all_factors[:, :width]
    new_a = lax.dynamic_slice_in_dim(all_factors, width + data_index * slice_width, slice_width, 1)
    factor_product = jnp.dot(new_b.T, new_a, preferred_element_type=jnp.float32)
    merged = (frozen_up_weight[0].astype(jnp.float32) + low_rank_scale * factor_product).astype(
        jnp.bfloat16
    )
    return (merged[None], renewed[None])


def frame_fits(nz, nx, width, block, slice_width):
    if nx != 2 or nz < 3 or nz > 8 or block % 128 != 64 or block < 192 or width % 512 or slice_width % 128:
        return False
    for row in range(nz):
        for column in range(2):
            begin = row * 2 * block + column * (block - 64)
            if begin < width < begin + block - 64:
                return False
    return True


def solution(mesh):
    nz, nx = mesh.shape["wide"], mesh.shape["dp"]

    def per_device(tokens, cotangent, frozen_up_weight, master, moment_one, moment_two):
        args = (tokens, cotangent, frozen_up_weight, master, moment_one, moment_two)
        if frame_fits(nz, nx, tokens.shape[2], master.shape[2], frozen_up_weight.shape[2]):
            return fused_shards(nz, *args)
        return shards(*args)

    in_specs = (
        P("expert", ("groups", "wide", "dp"), None),
        P("expert", ("groups", "wide", "dp"), None),
        P("expert", None, "dp"),
        P(("groups", "expert"), None, ("wide", "dp")),
        P(("groups", "expert"), None, ("wide", "dp")),
        P(("groups", "expert"), None, ("wide", "dp")),
    )
    out_specs = (P(("groups", "expert"), None, "dp"), P(("groups", "expert"), None, ("wide", "dp")))
    return jax.shard_map(per_device, mesh=mesh, in_specs=in_specs, out_specs=out_specs, check_vma=False)
```

```python
import functools

import jax
import jax.numpy as jnp
from jax import lax
from jax.experimental import pallas as pl
from jax.experimental.pallas import tpu as pltpu
from jax.sharding import PartitionSpec as P

beta_one = 0.9
beta_two = 0.95
learn_rate = 0.01
weight_decay = 0.1
step_count = 10
eps_adam = 1e-08
low_rank_scale = 2.0

MESH = pl.DeviceIdType.MESH
DIRECT = 1
NT = (((1,), (1,)), ((), ()))
TN = (((0,), (0,)), ((), ()))


def adam(master, moment_one, moment_two, gradient):
    first_new = beta_one * moment_one + (1.0 - beta_one) * gradient
    second_new = beta_two * moment_two + (1.0 - beta_two) * gradient * gradient
    step_size = (
        first_new
        / (1.0 - beta_one**step_count)
        / (jnp.sqrt(second_new / (1.0 - beta_two**step_count)) + eps_adam)
    )
    return master - learn_rate * (step_size + weight_decay * master)


def update_kernel(
    nz, scale, tok, cot, mas_hbm, mom1_hbm, mom2_hbm, weight, ren, out_b, out_a, held,
    both, mas, mom1, mom2, frame, gat, fac, snd_x, rcv_x, own, snd_z, rcv_z, straight, allf,
    in_sem, g_send, g_recv, x_send, x_recv, z_send, z_recv, f_send, f_recv,
):
    width = tok.shape[2]
    hidden_units = cot.shape[2]
    rank, block = mas.shape[1], mas.shape[2]
    lanes = gat.shape[3]
    main = lanes - 128
    pair = 2 * block
    shift = lanes - block
    z = lax.axis_index("wide")
    x = lax.axis_index("dp")
    xo = 1 - x

    def z_at(distance):
        return lax.rem(z + distance, nz)

    in_tok = pltpu.make_async_copy(tok.at[0], both.at[:, pl.ds(0, width)], in_sem.at[0])
    in_cot = pltpu.make_async_copy(cot.at[0], both.at[:, pl.ds(width, hidden_units)], in_sem.at[1])
    in_mas = pltpu.make_async_copy(mas_hbm, mas, in_sem.at[2])
    in_mom1 = pltpu.make_async_copy(mom1_hbm, mom1, in_sem.at[3])
    in_mom2 = pltpu.make_async_copy(mom2_hbm, mom2, in_sem.at[4])
    in_weight = pltpu.make_async_copy(weight, held, in_sem.at[5])
    for copy in (in_mas, in_tok, in_cot, in_mom1, in_mom2, in_weight):
        copy.start()

    barrier = pltpu.get_barrier_semaphore()
    for d in range(1, nz):
        pl.semaphore_signal(barrier, inc=1, device_id={"wide": z_at(d)}, device_id_type=MESH)
    pl.semaphore_signal(barrier, inc=1, device_id={"dp": xo}, device_id_type=MESH)
    for d in (1, nz - 1):
        pl.semaphore_signal(barrier, inc=1, device_id={"wide": z_at(d), "dp": xo}, device_id_type=MESH)

    def framed(ref):
        frame[:, main:] = jnp.zeros((rank, 128), jnp.float32)
        frame[:, :block] = ref[0]
        return pltpu.roll(frame[...], x * shift, 1)

    in_mas.wait()
    master = framed(mas)
    gat[x, z] = master.astype(jnp.bfloat16)
    pl.semaphore_wait(barrier, nz + 2)

    def share(buf, send, recv):
        targets = [(z_at(d), x) for d in range(2, nz)] + [(z, xo), (z_at(1), xo), (z_at(1), x)]
        sends = []
        for i, (row, column) in enumerate(targets):
            sends.append(pltpu.make_async_remote_copy(
                buf.at[x, z], buf.at[x, z], send.at[i], recv.at[x, z],
                device_id={"wide": row, "dp": column}, device_id_type=MESH))
        for copy in sends:
            copy.start()
        return sends

    def arrived(buf, recv, column, row):
        pltpu.make_async_remote_copy(
            buf.at[column, row], buf.at[column, row], recv.at[column, row], recv.at[column, row],
            device_id={"dp": xo}, device_id_type=MESH).wait_recv()

    def forward(buf, send, recv, d):
        row = z_at(nz - d)
        arrived(buf, recv, x, row)
        copy = pltpu.make_async_remote_copy(
            buf.at[x, row], buf.at[x, row], send.at[nz - 1 + d], recv.at[x, row],
            device_id={"dp": xo}, device_id_type=MESH)
        copy.start()
        return copy

    def start_of(row, column):
        return row * pair + column * main_step

    main_step = block - shift

    def is_b(row, column):
        begin = start_of(row, column)
        return begin < width, begin + main < width

    sends = share(gat, g_send, g_recv)
    in_tok.wait()
    in_cot.wait()

    hidden = jnp.zeros((rank, both.shape[0]), jnp.float32)
    back = jnp.zeros((rank, both.shape[0]), jnp.float32)

    def project(row, column, hidden, back):
        begin = start_of(row, column)
        b_main, b_last = is_b(row, column)
        part = lax.dot_general(
            gat[column, row, :, :main], both[:, pl.ds(pl.multiple_of(begin, 128), main)],
            NT, preferred_element_type=jnp.float32)
        last = lax.dot_general(
            gat[column, row, :, main:], both[:, pl.ds(pl.multiple_of(begin + main, 128), 128)],
            NT, preferred_element_type=jnp.float32)
        hidden = hidden + jnp.where(b_main, part, 0.0) + jnp.where(b_last, last, 0.0)
        back = back + jnp.where(b_main, 0.0, part) + jnp.where(b_last, 0.0, last)
        return hidden, back

    hidden, back = project(z, x, hidden, back)
    for d in range(2, nz):
        sends.append(forward(gat, g_send, g_recv, d))
        hidden, back = project(z_at(nz - d), x, hidden, back)
    arrived(gat, g_recv, x, z_at(nz - 1))
    hidden, back = project(z_at(nz - 1), x, hidden, back)
    for d in range(nz):
        row = z_at(nz - d)
        arrived(gat, g_recv, xo, row)
        hidden, back = project(row, xo, hidden, back)
    hidden = hidden.astype(jnp.bfloat16).astype(jnp.float32)
    back = back.astype(jnp.bfloat16).astype(jnp.float32)

    def gradient(row, column):
        begin = start_of(row, column)
        b_main, b_last = is_b(row, column)
        part = jnp.dot(
            jnp.where(b_main, back, hidden).astype(jnp.bfloat16),
            both[:, pl.ds(pl.multiple_of(begin, 128), main)], preferred_element_type=jnp.float32)
        last = jnp.dot(
            jnp.where(b_last, back, hidden).astype(jnp.bfloat16),
            both[:, pl.ds(pl.multiple_of(begin + main, 128), 128)], preferred_element_type=jnp.float32)
        return part, last

    direct = DIRECT % nz
    order = [d for d in range(nz - 1, 0, -1) if d != direct] + [direct, 0]
    x_copies = []
    for i, d in enumerate(order):
        row = z_at(d)
        target = {"wide": row, "dp": xo} if d == direct else {"dp": xo}
        part, last = gradient(row, xo)
        snd_x[i, :, :main] = part.astype(jnp.bfloat16)
        snd_x[i, :, main:] = last.astype(jnp.bfloat16)
        landing = straight if d == direct else rcv_x.at[i]
        copy = pltpu.make_async_remote_copy(
            snd_x.at[i], landing, x_send.at[i], x_recv.at[i],
            device_id=target, device_id_type=MESH)
        copy.start()
        x_copies.append(copy)
    for i, d in enumerate(order):
        part, last = gradient(z_at(d), x)
        own[i, :, :main] = part
        own[i, :, main:] = last

    in_mom1.wait()
    in_mom2.wait()
    moment_one = framed(mom1)
    moment_two = framed(mom2)

    z_copies = []
    for i in (nz - 2, *range(nz - 2)):
        row = z_at(order[i])
        part = own[i]
        if order[i] != direct:
            x_copies[i].wait_recv()
            part = part + rcv_x[i].astype(jnp.float32)
        snd_z[i] = part.astype(jnp.bfloat16)
        copy = pltpu.make_async_remote_copy(
            snd_z.at[i], rcv_z.at[z], z_send.at[i], z_recv.at[z],
            device_id={"wide": row}, device_id_type=MESH)
        copy.start()
        z_copies.append(copy)
    x_copies[nz - 1].wait_recv()
    x_copies[nz - 2].wait_recv()
    total = own[nz - 1] + rcv_x[nz - 1].astype(jnp.float32) + straight[...].astype(jnp.float32)
    for d in range(1, nz):
        row = z_at(nz - d)
        pltpu.make_async_remote_copy(
            snd_z.at[d - 1], rcv_z.at[row], z_send.at[d - 1], z_recv.at[row],
            device_id={"wide": row}, device_id_type=MESH).wait_recv()
        total = total + rcv_z[row].astype(jnp.float32)

    renewed = adam(master, moment_one, moment_two, total * scale)
    lane = lax.broadcasted_iota(jnp.int32, (rank, lanes), 1)
    first = x * shift
    valid = (lane >= first) & (lane < first + block)
    fac[x, z] = jnp.where(valid, renewed, 0.0).astype(jnp.bfloat16)
    sends += share(fac, f_send, f_recv)
    frame[...] = pltpu.roll(renewed, lanes - x * shift, 1)
    ren[0] = frame[:, :block]

    for d in range(2, nz):
        sends.append(forward(fac, f_send, f_recv, d))
    arrived(fac, f_recv, x, z_at(nz - 1))
    for d in range(nz):
        arrived(fac, f_recv, xo, z_at(nz - d))
    for row in range(nz):
        base = row * pair
        allf[:, base:base + main] = fac[0, row, :, :main]
        joined = fac[0, row, :, main:].astype(jnp.float32) + fac[1, row, :, :128].astype(jnp.float32)
        allf[:, base + main:base + lanes] = joined.astype(jnp.bfloat16)
        allf[:, base + lanes:base + pair] = fac[1, row, :, 128:]
    slice_width = out_a.shape[1]
    out_b[...] = allf[:, :width]
    mine = allf[:, pl.ds(pl.multiple_of(width + x * slice_width, 128), slice_width)]
    out_a[...] = (mine.astype(jnp.float32) * low_rank_scale).astype(jnp.bfloat16)
    for copy in sends + x_copies + z_copies:
        copy.wait_send()
    in_weight.wait()


def merge_kernel(step, weight, new_b, new_a, ren, merged, ren_out, staged, sem):
    ren_copy = pltpu.make_async_copy(ren, ren_out, sem.at[0])
    ren_copy.start()
    copies = []
    for i in range(staged.shape[0] // step):
        part = pl.ds(i * step, step)
        product = lax.dot_general(new_b[:, part], new_a[...], TN, preferred_element_type=jnp.float32)
        staged[part] = (weight[0, part].astype(jnp.float32) + product).astype(jnp.bfloat16)
        copy = pltpu.make_async_copy(staged.at[part], merged.at[0, part], sem.at[i + 1])
        copy.start()
        copies.append(copy)
    for copy in copies + [ren_copy]:
        copy.wait()


def fused_shards(nz, tokens, cotangent, frozen_up_weight, master, moment_one, moment_two):
    rows, width = tokens.shape[1:]
    hidden_units = cotangent.shape[2]
    rank, block = master.shape[1:]
    slice_width = frozen_up_weight.shape[2]
    lanes = block + 64
    bf16, f32 = jnp.bfloat16, jnp.float32
    vmem = pl.BlockSpec(memory_space=pltpu.VMEM)
    hbm = pl.BlockSpec(memory_space=pltpu.HBM)
    dma = pltpu.SemaphoreType.DMA
    scale = low_rank_scale / (rows * nz * 2)
    renewed, new_b, new_a, held = pl.pallas_call(
        functools.partial(update_kernel, nz, scale),
        out_shape=(
            pltpu.VMEM(master.shape, f32),
            pltpu.VMEM((rank, width), bf16),
            pltpu.VMEM((rank, slice_width), bf16),
            pltpu.VMEM(frozen_up_weight.shape, bf16),
        ),
        in_specs=[hbm] * 6,
        out_specs=(vmem,) * 4,
        scratch_shapes=[
            pltpu.VMEM((rows, width + hidden_units), bf16),
            pltpu.VMEM(master.shape, f32),
            pltpu.VMEM(master.shape, f32),
            pltpu.VMEM(master.shape, f32),
            pltpu.VMEM((rank, lanes), f32),
            pltpu.VMEM((2, nz, rank, lanes), bf16),
            pltpu.VMEM((2, nz, rank, lanes), bf16),
            pltpu.VMEM((nz, rank, lanes), bf16),
            pltpu.VMEM((nz, rank, lanes), bf16),
            pltpu.VMEM((nz, rank, lanes), f32),
            pltpu.VMEM((nz - 1, rank, lanes), bf16),
            pltpu.VMEM((nz, rank, lanes), bf16),
            pltpu.VMEM((rank, lanes), bf16),
            pltpu.VMEM((rank, width + hidden_units), bf16),
            dma((6,)),
            dma((2 * nz,)),
            dma((2, nz)),
            dma((nz,)),
            dma((nz,)),
            dma((nz - 1,)),
            dma((nz,)),
            dma((2 * nz,)),
            dma((2, nz)),
        ],
        compiler_params=pltpu.CompilerParams(
            collective_id=0, has_side_effects=True, vmem_limit_bytes=56 * 1024 * 1024
        ),
    )(tokens, cotangent, master, moment_one, moment_two, frozen_up_weight)
    step = 256
    merged, renewed = pl.pallas_call(
        functools.partial(merge_kernel, step),
        out_shape=(
            jax.ShapeDtypeStruct(frozen_up_weight.shape, bf16),
            jax.ShapeDtypeStruct(master.shape, f32),
        ),
        in_specs=[vmem] * 4,
        out_specs=(hbm, hbm),
        scratch_shapes=[pltpu.VMEM((width, slice_width), bf16), dma((width // step + 1,))],
        compiler_params=pltpu.CompilerParams(vmem_limit_bytes=20 * 1024 * 1024),
    )(held, new_b, new_a, renewed)
    return merged, renewed


def shards(tokens, cotangent, frozen_up_weight, master, moment_one, moment_two):
    wide_count = lax.axis_size("wide")
    data_count = lax.axis_size("dp")
    width = tokens.shape[2]
    inputs = tokens[0]
    upstream = cotangent[0]
    current = master[0].astype(jnp.bfloat16)
    gathered = lax.all_gather(current, ("wide", "dp"), axis=1, tiled=True)
    rows_b = gathered[:, :width]
    cols_a = gathered[:, width:]
    hidden = jnp.dot(inputs, rows_b.T, preferred_element_type=jnp.float32).astype(jnp.bfloat16)
    back = jnp.dot(upstream, cols_a.T, preferred_element_type=jnp.float32).astype(jnp.bfloat16)
    up_factor = jnp.dot(back.T, inputs, preferred_element_type=jnp.float32)
    down_factor = jnp.dot(hidden.T, upstream, preferred_element_type=jnp.float32)
    partial_value = jnp.concatenate([up_factor, down_factor], axis=1)
    reduced_total = lax.psum_scatter(partial_value, ("wide", "dp"), scatter_dimension=1, tiled=True)
    gathered_rows = inputs.shape[0] * wide_count * data_count
    adapter_gradient = reduced_total * (low_rank_scale / gathered_rows)
    renewed = adam(master[0], moment_one[0], moment_two[0], adapter_gradient)
    factors = renewed.astype(jnp.bfloat16)
    all_factors = lax.all_gather(factors, ("wide", "dp"), axis=1, tiled=True)
    slice_width = frozen_up_weight.shape[2]
    data_index = lax.axis_index("dp")
    new_b = all_factors[:, :width]
    new_a = lax.dynamic_slice_in_dim(all_factors, width + data_index * slice_width, slice_width, 1)
    factor_product = jnp.dot(new_b.T, new_a, preferred_element_type=jnp.float32)
    merged = (frozen_up_weight[0].astype(jnp.float32) + low_rank_scale * factor_product).astype(
        jnp.bfloat16
    )
    return (merged[None], renewed[None])


def frame_fits(nz, nx, width, block, slice_width):
    if nx != 2 or nz < 3 or nz > 8 or block % 128 != 64 or block < 192 or width % 512 or slice_width % 128:
        return False
    for row in range(nz):
        for column in range(2):
            begin = row * 2 * block + column * (block - 64)
            if begin < width < begin + block - 64:
                return False
    return True


def solution(mesh):
    nz, nx = mesh.shape["wide"], mesh.shape["dp"]

    def per_device(tokens, cotangent, frozen_up_weight, master, moment_one, moment_two):
        args = (tokens, cotangent, frozen_up_weight, master, moment_one, moment_two)
        if frame_fits(nz, nx, tokens.shape[2], master.shape[2], frozen_up_weight.shape[2]):
            return fused_shards(nz, *args)
        return shards(*args)

    in_specs = (
        P("expert", ("groups", "wide", "dp"), None),
        P("expert", ("groups", "wide", "dp"), None),
        P("expert", None, "dp"),
        P(("groups", "expert"), None, ("wide", "dp")),
        P(("groups", "expert"), None, ("wide", "dp")),
        P(("groups", "expert"), None, ("wide", "dp")),
    )
    out_specs = (P(("groups", "expert"), None, "dp"), P(("groups", "expert"), None, ("wide", "dp")))
    return jax.shard_map(per_device, mesh=mesh, in_specs=in_specs, out_specs=out_specs, check_vma=False)
```
